32 devices in a mesh: gx: 4 (over y, x), gy: 4 (over z), gz: 2 (over core).
Axes of the slice: x: 2, y: 2, z: 4, core: 2. Of those that a mesh axis runs over, the one named last changes fastest.
Arguments:
- displacement: bfloat16 [16, 4, 4, 12, 3, 32, 128], P('gx', 'gy', 'gz'), may hold values from -96 to 96
- dof_weight: bfloat16 [16, 4, 4, 12, 128], P('gx', 'gy', 'gz'), may hold values from 0.099609375 to 10
- coarse_matrix: float32 [16, 4, 4, 27, 36, 36], P('gx', 'gy', 'gz'), may hold values from -48 to 48, as said below
- block_inverse: float32 [16, 4, 4, 36, 36], P('gx', 'gy', 'gz'), may hold values from -12 to 12, as said below
Outputs:
- edge_average: float32 [16, 4, 4, 12, 3, 32], P('gx', 'gy', 'gz')
- coarse_solution: float32 [16, 4, 4, 36, 32], P('gx', 'gy', 'gz')
The draws below stay inside these ranges and needn't reach their ends.
Inputs may be any that keep to these rules, and one draw needn't show every extreme that they name: coarse_matrix is the replicated form of one operator over edge unknowns: rows of the same edge seen from its four subdomains are equal, and each column of an edge is stored at exactly one of that edge's subdomains (zeros at the others). block_inverse[p] is block-diagonal in 3 x 3 blocks, each the inverse of the matching diagonal 3 x 3 block of coarse_matrix[p, 13].
All inputs are finite; a program needn't handle non-finite values.
Results may differ from the reference program's by a relative error of at most 0.0003.
Values sent between devices are 32-bit elements; how exact they have to be, the bound alone decides.
A program may use at most 64 MiB of HBM per device.

```python
import math
import jax
import jax.numpy as jnp
import numpy as np
from jax import lax

RHS = 32
EDGES = 12
COMP = 3
DOFS = 128
SWEEPS = 4
COARSE = 36
NX = 16
NY = 4
NZ = 4


edge_offsets = np.array([[0, 0, 0], [0, 0, 1], [0, 1, 0], [0, 1, 1], [0, 0, 0], [0, 0, 1], [1, 0, 0], [1, 0, 1], [0, 0, 0], [0, 1, 0], [1, 0, 0], [1, 1, 0]])


def owner_mask():
    table = np.zeros((27, 9, 9), np.float32)
    for offset in range(27):
        delta = [offset // 9 - 1, offset // 3 % 3 - 1, offset % 3 - 1]
        for row_dir in range(3):
            for col_dir in range(3):
                if row_dir == col_dir or delta[col_dir] <= 0:
                    table[offset, 3 * row_dir:3 * row_dir + 3, 3 * col_dir:3 * col_dir + 3] = 1.0
    return table


def placement_table():
    table = np.full((12, 27, 12), 81, np.int32)
    for edge in range(12):
        row_dir = edge // 4
        anchor = edge_offsets[edge]
        for offset in range(27):
            delta = [offset // 9 - 1, offset // 3 % 3 - 1, offset % 3 - 1]
            for col_dir in range(3):
                if not (row_dir == col_dir or delta[col_dir] <= 0):
                    continue
                target = []
                for comp in range(3):
                    if comp == col_dir:
                        target.append(0)
                    else:
                        target.append(1 if anchor[comp] + delta[comp] >= 1 else 0)
                other = -1
                for cand in range(4 * col_dir, 4 * col_dir + 4):
                    if list(edge_offsets[cand]) == target:
                        other = cand
                place = [anchor[comp] + delta[comp] - target[comp] for comp in range(3)]
                stored = 9 * (place[0] + 1) + 3 * (place[1] + 1) + (place[2] + 1)
                table[edge, stored, other] = 3 * offset + col_dir
    return table


def coarse_pair(key):
    base_key = jax.random.fold_in(key, 7)
    noise_key, scale_key = jax.random.split(base_key)
    noise = jax.random.normal(noise_key, (NX, NY, NZ, 27, 9, 9), jnp.float32) * 0.03
    noise = noise * jnp.asarray(owner_mask())
    blocks = noise.at[:, :, :, 13].add(2.0 * jnp.eye(9, dtype=jnp.float32))
    spread = math.log(2.0)
    scales = jnp.exp(jax.random.uniform(scale_key, (NX, NY, NZ, 9), jnp.float32, -spread, spread))
    column_list = []
    for offset in range(27):
        shift_x = offset // 9 - 1
        shift_y = offset // 3 % 3 - 1
        shift_z = offset % 3 - 1
        column_list.append(jnp.roll(scales, (-shift_x, -shift_y, -shift_z), (0, 1, 2)))
    columns = jnp.stack(column_list, 3)
    owned = scales[:, :, :, None, :, None] * blocks * columns[:, :, :, :, None, :]
    diag_list = []
    for direction in range(3):
        diag_list.append(jnp.linalg.inv(owned[:, :, :, 13, 3 * direction:3 * direction + 3, 3 * direction:3 * direction + 3]))
    diag_inverse = jnp.stack(diag_list, 3)
    table = placement_table()
    row_blocks = []
    inverse_blocks = []
    for edge in range(12):
        row_dir = edge // 4
        anchor = edge_offsets[edge]
        rolled = jnp.roll(owned, (-int(anchor[0]), -int(anchor[1]), -int(anchor[2])), (0, 1, 2))
        rows = rolled[:, :, :, :, 3 * row_dir:3 * row_dir + 3, :]
        rows = rows.reshape(NX, NY, NZ, 27, 3, 3, 3)
        rows = jnp.transpose(rows, (0, 1, 2, 3, 5, 4, 6)).reshape(NX, NY, NZ, 81, 3, 3)
        rows = jnp.concatenate([rows, jnp.zeros((NX, NY, NZ, 1, 3, 3), jnp.float32)], 3)
        picked = jnp.take(rows, jnp.asarray(table[edge]).reshape(-1), axis=3)
        picked = picked.reshape(NX, NY, NZ, 27, 12, 3, 3)
        picked = jnp.transpose(picked, (0, 1, 2, 3, 5, 4, 6)).reshape(NX, NY, NZ, 27, 3, 36)
        row_blocks.append(picked)
        rolled_inverse = jnp.roll(diag_inverse, (-int(anchor[0]), -int(anchor[1]), -int(anchor[2])), (0, 1, 2))
        inverse_blocks.append(rolled_inverse[:, :, :, row_dir])
    matrix = jnp.stack(row_blocks, 4).reshape(NX, NY, NZ, 27, 36, 36)
    stacked = jnp.stack(inverse_blocks, 3)
    inverse = jnp.einsum('xyzeab,ef->xyzeafb', stacked, jnp.eye(12, dtype=jnp.float32)).reshape(NX, NY, NZ, 36, 36)
    return (matrix, inverse)


def draw_coarse_matrix(key, part):
    return coarse_pair(key)[0]


def draw_block_inverse(key, part):
    return coarse_pair(key)[1]


def level_of(key, extent, shards, low, largest):
    def one(position, blocks):
        steps = jax.random.uniform(jax.random.fold_in(jax.random.fold_in(key, 6), position), (blocks,), jnp.float32, low / len(shards), largest / len(shards))
        return jnp.repeat(jnp.exp(steps), extent[position] // blocks).reshape((-1,) + (1,) * (len(extent) - position - 1))

    factor_of = one(*shards[0])
    for cut in shards[1:]:
        factor_of = factor_of * one(*cut)
    return factor_of


def centred(stream_key, shape, scale, limit, pieces=(), kind=jnp.bfloat16):
    entries = jax.random.normal(stream_key, shape, jnp.float32) * scale
    if len(pieces) > 0:
        entries = level_of(stream_key, shape, pieces, -0.22, 0.18) * entries
    return jnp.clip(entries, min=-limit, max=limit).astype(kind)


def setup_inputs(seed: int = 0) -> dict:
    streams_of = jax.random.split(jax.random.key(seed), 5)
    return {
        "displacement": centred(streams_of[0], (NX, NY, NZ, EDGES, COMP, RHS, DOFS), 16.0, 96.0, ((0, 4), (1, 4), (2, 2))),
        "dof_weight": jnp.clip(jnp.exp(math.log(10.0) - 4.609084 * jax.random.uniform(streams_of[1], (NX, NY, NZ, EDGES, DOFS), jnp.float32) ** level_of(streams_of[1], (NX, NY, NZ, EDGES, DOFS), ((0, 4), (1, 4), (2, 2)), -0.2, 0.2)), 0.099609375, 10.0).astype(jnp.bfloat16),
        "coarse_matrix": draw_coarse_matrix(jax.random.fold_in(streams_of[4], 71), 0),
        "block_inverse": draw_block_inverse(jax.random.fold_in(streams_of[4], 71), 0),
    }


edge_offsets = np.array([[0, 0, 0], [0, 0, 1], [0, 1, 0], [0, 1, 1], [0, 0, 0], [0, 0, 1], [1, 0, 0], [1, 0, 1], [0, 0, 0], [0, 1, 0], [1, 0, 0], [1, 1, 0]])

def combine(padded_numer, padded_weight, size_x, size_y, size_z):
    numer_list = []
    weight_list = []
    for edge in range(12):
        first = 4 * (edge // 4)
        numer_total = 0.0
        weight_total = 0.0
        for other in range(first, first + 4):
            delta = edge_offsets[edge] - edge_offsets[other]
            start_x = 1 + int(delta[0])
            start_y = 1 + int(delta[1])
            start_z = 1 + int(delta[2])
            numer_total = numer_total + padded_numer[start_x:start_x + size_x, start_y:start_y + size_y, start_z:start_z + size_z, other]
            weight_total = weight_total + padded_weight[start_x:start_x + size_x, start_y:start_y + size_y, start_z:start_z + size_z, other]
        numer_list.append(numer_total)
        weight_list.append(weight_total)
    return jnp.stack(numer_list, 3) / jnp.stack(weight_list, 3)[..., None, None]

def apply_matrix(padded, coarse_matrix, size_x, size_y, size_z):
    total = jnp.zeros((size_x, size_y, size_z) + padded.shape[3:], jnp.float32)
    for offset in range(27):
        start_x = offset // 9
        start_y = offset // 3 % 3
        start_z = offset % 3
        piece = padded[start_x:start_x + size_x, start_y:start_y + size_y, start_z:start_z + size_z]
        total = total + jnp.einsum('xyzij,xyzjr->xyzir', coarse_matrix[:, :, :, offset], piece, precision=lax.Precision.HIGHEST)
    return total

def reference(displacement, dof_weight, coarse_matrix, block_inverse):
    size_x, size_y, size_z = (displacement.shape[0], displacement.shape[1], displacement.shape[2])
    numers = jnp.einsum('xyzecrk,xyzek->xyzecr', displacement.astype(jnp.float32), dof_weight.astype(jnp.float32))
    weights = jnp.sum(dof_weight.astype(jnp.float32), axis=-1)
    padded_numer = jnp.pad(numers, ((1, 1), (1, 1), (1, 1), (0, 0), (0, 0), (0, 0)), mode='wrap')
    padded_weight = jnp.pad(weights, ((1, 1), (1, 1), (1, 1), (0, 0)), mode='wrap')
    averages = combine(padded_numer, padded_weight, size_x, size_y, size_z)
    rhs_rows = averages.reshape(size_x, size_y, size_z, COARSE, averages.shape[-1])
    iterate = jnp.einsum('xyzij,xyzjr->xyzir', block_inverse, rhs_rows, precision=lax.Precision.HIGHEST)
    for sweep in range(SWEEPS - 1):
        padded = jnp.pad(iterate, ((1, 1), (1, 1), (1, 1), (0, 0), (0, 0)), mode='wrap')
        product = apply_matrix(padded, coarse_matrix, size_x, size_y, size_z)
        iterate = iterate + jnp.einsum('xyzij,xyzjr->xyzir', block_inverse, rhs_rows - product, precision=lax.Precision.HIGHEST)
    return (averages, iterate)
```

```python
import functools
import itertools

import jax
import jax.numpy as jnp
import ml_dtypes
import numpy as np
from jax import lax
from jax.experimental import pallas as pl
from jax.experimental.pallas import tpu as pltpu
from jax.sharding import PartitionSpec as P

SWEEPS = 4
MESH = pl.DeviceIdType.MESH
F32 = jnp.float32
BF16 = jnp.bfloat16
OFFSETS = [
    (0, 0, 0), (0, 0, 1), (0, 1, 0), (0, 1, 1),
    (0, 0, 0), (0, 0, 1), (1, 0, 0), (1, 0, 1),
    (0, 0, 0), (0, 1, 0), (1, 0, 0), (1, 1, 0),
]
STEPS = [(0, 0)] + [s for s in itertools.product((-1, 0, 1), (-1, 0, 1)) if s != (0, 0)]
SLOT = {s: i for i, s in enumerate(STEPS)}
HALF = 48


def site_row(edge, comp):
    oy = OFFSETS[edge][1]
    if edge < 4:
        return 3 * oy + comp
    if edge < 8:
        return (6, 7, 14)[comp]
    return 8 + 3 * oy + comp


def tables():
    place = np.zeros((36, 64), np.float32)
    spread = np.zeros((64, 12), np.float32)
    chunk = np.full((64, 128), -1, np.int32)
    fold = np.zeros((3, 108, 256), np.float32)
    order = np.zeros((HALF, 36), np.float32)
    rest = 16
    for edge in range(12):
        ox, oy, oz = OFFSETS[edge]
        for comp in range(3):
            row = 3 * edge + comp
            site = site_row(edge, comp)
            wide = 16 * (2 * ox + oz) + site
            place[row, wide] = 1
            spread[wide, edge] = 1
            chunk[wide] = row - np.arange(128) // 32
            for dx in range(3):
                for dz in range(3):
                    fold[dx, 36 * dz + row, 64 * (dx + ox) + 16 * (dz + oz) + site] = 1
            if ox == 0 and oz == 0:
                order[site, row] = 1
            else:
                order[rest, row] = 1
                rest += 1
    kind = ml_dtypes.bfloat16
    return (place.astype(kind), spread.astype(kind), chunk, fold.astype(kind),
            order.astype(kind), np.ascontiguousarray(order.T).astype(kind))


def split(value):
    high = value.astype(BF16)
    return high, (value - high.astype(F32)).astype(BF16)


def dot(a, b):
    return jnp.dot(a, b, preferred_element_type=F32)


def kernel(sizes, disp_hbm, weight_ref, matrix_hbm, inverse_ref, place_ref, spread_ref, chunk_ref,
           fold_ref, order_ref, back_ref, average_ref, result_ref,
           disp, matrix, operator, main, rim, zsend, zgot, sites, below, above, rows, wide,
           load_sem, send_sem, got_sem):
    nx, nz = 4, 2
    gx, gy, gz = (lax.axis_index(a) for a in ("gx", "gy", "gz"))
    cx, cy, cz = sizes

    def at(dx, dy, dz):
        return (lax.rem(gx + dx + cx, cx), lax.rem(gy + dy + cy, cy), lax.rem(gz + dz + cz, cz))

    load_disp = pltpu.make_async_copy(disp_hbm, disp, load_sem.at[0])
    load_matrix = pltpu.make_async_copy(matrix_hbm, matrix, load_sem.at[1])
    load_disp.start()
    load_matrix.start()
    barrier = pltpu.get_barrier_semaphore()
    for dx, dy in STEPS[1:]:
        pl.semaphore_signal(barrier, inc=1, device_id=at(dx, dy, 0), device_id_type=MESH)
    for dz in (-1, 1):
        pl.semaphore_signal(barrier, inc=1, device_id=at(0, 0, dz), device_id_type=MESH)

    lane = lax.broadcasted_iota(jnp.int32, (16, 128), 1)
    row = lax.broadcasted_iota(jnp.int32, (16, 128), 0)
    part = lane // 32
    ones = jnp.ones((128, 128), BF16)
    zero = jnp.zeros((16, 128), F32)

    load_disp.wait()
    number = {}
    mass = {}
    for cell in range(nx * nz):
        weight = dot(spread_ref[...], weight_ref[cell]).astype(BF16)
        full = lax.dot_general(weight, disp[cell], (((1,), (1,)), ((), ())),
                               preferred_element_type=F32)
        total = jnp.zeros((64, 128), F32)
        for t in range(9):
            total = total + jnp.where(chunk_ref[...] == 4 * t, full[:, 128 * t:128 * t + 128], 0.0)
        total = total + pltpu.roll(total, 64, 1)
        total = total + pltpu.roll(total, 32, 1)
        number[cell] = total
        mass[cell] = dot(weight, ones)
    for zs in range(nz + 1):
        body = zero
        edge = zero
        for oz in range(2):
            z = zs - oz
            if not 0 <= z < nz:
                continue
            for x in range(nx):
                for ox in range(2):
                    b = 16 * (2 * ox + oz)
                    value = number[x * nz + z][b:b + 16]
                    if x + ox < nx:
                        body = body + jnp.where(part == x + ox, value, 0.0)
                    else:
                        edge = edge + jnp.where(part == 0, value, 0.0)
                    heavy = mass[x * nz + z][b:b + 16]
                    edge = edge + jnp.where(lane // 8 == 4 + x + ox, heavy, 0.0)
        main[1, zs] = body
        rim[0, zs] = edge + jnp.where(part == 3, pltpu.roll(body, 96, 1), 0.0)

    pl.semaphore_wait(barrier, 10)
    copies = []
    for i, (dx, dy) in enumerate(STEPS):
        if i == 0:
            continue
        slot = SLOT[(-dx, -dy)]
        copies.append(pltpu.make_async_remote_copy(
            rim.at[0], rim.at[slot], send_sem.at[0, i], got_sem.at[0, slot],
            device_id=at(dx, dy, 0), device_id_type=MESH))
        if dx == 0:
            copies.append(pltpu.make_async_remote_copy(
                main.at[1], main.at[1 - dy], send_sem.at[0, 11 + (dy + 1) // 2],
                got_sem.at[0, 11 + (1 - dy) // 2],
                device_id=at(dx, dy, 0), device_id_type=MESH))
    for copy in copies:
        copy.start()

    load_matrix.wait()

    def prepare(cell, carry):
        base_high, base_low = split(inverse_ref[cell])
        base_high = dot(order_ref[...], base_high).astype(BF16)
        base_low = dot(order_ref[...], base_low).astype(BF16)
        for dy in range(3):
            sum_high = jnp.zeros((36, 256), F32)
            sum_low = jnp.zeros((36, 256), F32)
            for dx in range(3):
                first = 27 * cell + 9 * dx + 3 * dy
                joined = jnp.concatenate([matrix[first + k] for k in range(3)], axis=1)
                high, low = split(joined)
                sum_high = sum_high + dot(high, fold_ref[dx])
                sum_low = sum_low + dot(low, fold_ref[dx])
            sum_high = sum_high.astype(BF16)
            sum_low = sum_low.astype(BF16)
            scaled = dot(base_high, sum_high) + dot(base_low, sum_high) + dot(base_high, sum_low)
            high, low = split(scaled)
            operator[cell, dy, :HALF] = high
            operator[cell, dy, HALF:] = low
        return carry

    lax.fori_loop(0, nx * nz, prepare, 0)

    for copy in copies:
        copy.wait()

    lower = (row % 8) < 3
    upper = ((row % 8) >= 3) & ((row % 8) < 6)
    for zs in range(nz + 1):
        sums = {}
        for dy in (-1, 0, 1):
            before = rim[SLOT[(-1, dy)], zs]
            after = pltpu.roll(rim[SLOT[(1, dy)], zs], 32, 1)
            body = main[1 + dy, zs] + jnp.where(part == 0, before, 0.0)
            edge = (rim[SLOT[(0, dy)], zs]
                    + jnp.where(lane // 8 == 4, pltpu.roll(before, 96, 1), 0.0)
                    + jnp.where((part == 0) | (lane // 8 == 8), after, 0.0))
            sums[dy] = (body, edge)
        for k in range(2):
            zsend[zs, k] = (sums[0][k]
                            + jnp.where(lower, pltpu.roll(sums[-1][k], 13, 0), 0.0)
                            + jnp.where(upper, pltpu.roll(sums[1][k], 3, 0), 0.0))
    copies = [
        pltpu.make_async_remote_copy(zsend.at[nz], zgot.at[0], send_sem.at[0, 9], got_sem.at[0, 9],
                                     device_id=at(0, 0, 1), device_id_type=MESH),
        pltpu.make_async_remote_copy(zsend.at[0], zgot.at[1], send_sem.at[0, 10], got_sem.at[0, 10],
                                     device_id=at(0, 0, -1), device_id_type=MESH),
    ]
    for copy in copies:
        copy.start()
    for copy in copies:
        copy.wait()
    inner = []
    outer = []
    for zs in range(nz + 1):
        body = zsend[zs, 0]
        edge = zsend[zs, 1]
        if zs == 0:
            body, edge = body + zgot[0, 0], edge + zgot[0, 1]
        if zs == nz:
            body, edge = body + zgot[1, 0], edge + zgot[1, 1]
        heavy = zero
        for x in range(nx):
            heavy = jnp.where(part == x, edge[:, 32 + 8 * x:33 + 8 * x], heavy)
        last = jnp.broadcast_to(edge[:, 64:65], (16, 128))
        inner.append(body / jnp.where(heavy == 0.0, 1.0, heavy))
        edge = edge / jnp.where(last == 0.0, 1.0, last)
        outer.append(jnp.where(part == 3, pltpu.roll(edge, 96, 1), pltpu.roll(inner[-1], 96, 1)))

    def joined_split(value):
        high, low = split(value)
        return jnp.concatenate([high, low], axis=1)

    def store(ref, z, value):
        for x in range(nx):
            ref[x * nz + z] = value[:, 32 * x:32 * x + 32]

    wide_part = lax.broadcasted_iota(jnp.int32, (HALF, 128), 1) // 32
    start = []
    current = []
    for z in range(nz):
        wide[...] = jnp.concatenate([inner[z], inner[z + 1], outer[z], outer[z + 1]], axis=0)
        pair = joined_split(wide[...])
        cells = dot(place_ref[...], pair)
        cells = cells[:, :128] + cells[:, 128:]
        store(average_ref, z, cells)
        pair = joined_split(cells)
        value = jnp.zeros((HALF, 128), F32)
        for x in range(nx):
            base_high, base_low = split(inverse_ref[x * nz + z])
            base_high = dot(order_ref[...], base_high).astype(BF16)
            base_low = dot(order_ref[...], base_low).astype(BF16)
            whole = dot(base_high, pair)
            whole = whole[:, :128] + whole[:, 128:] + dot(base_low, pair[:, :128])
            value = jnp.where(wide_part == x, whole, value)
        start.append(value)
        current.append(value)

    for sweep in range(SWEEPS - 1):
        r = sweep + 1
        for z in range(nz):
            sites[sweep, 0, z] = current[z][:16]
        copies = []
        for i, (dx, dy) in enumerate(STEPS):
            if i == 0:
                continue
            slot = SLOT[(-dx, -dy)]
            copies.append(pltpu.make_async_remote_copy(
                sites.at[sweep, 0], sites.at[sweep, slot], send_sem.at[r, i], got_sem.at[r, slot],
                device_id=at(dx, dy, 0), device_id_type=MESH))
        for copy in copies:
            copy.start()
        for copy in copies:
            copy.wait()
        copies = [
            pltpu.make_async_remote_copy(
                sites.at[sweep, :, nz - 1], below.at[sweep], send_sem.at[r, 9], got_sem.at[r, 9],
                device_id=at(0, 0, 1), device_id_type=MESH),
            pltpu.make_async_remote_copy(
                sites.at[sweep], above.at[sweep], send_sem.at[r, 10], got_sem.at[r, 10],
                device_id=at(0, 0, -1), device_id_type=MESH),
        ]
        for copy in copies:
            copy.start()

        def gather(zs, load, sweep=sweep):
            for dy in (-1, 0, 1):
                own, before, after = (load(SLOT[(s, dy)]) for s in (0, -1, 1))
                shifted = [
                    jnp.where(part == 0, pltpu.roll(before, 32, 1), pltpu.roll(own, 32, 1)),
                    own,
                    jnp.where(part == 3, pltpu.roll(after, 96, 1), pltpu.roll(own, 96, 1)),
                    jnp.where(part >= 2, pltpu.roll(after, 64, 1), pltpu.roll(own, 64, 1)),
                ]
                for s in range(4):
                    high, low = split(shifted[s])
                    rows[dy + 1, s, zs, :, :128] = high
                    rows[dy + 1, s, zs, :, 128:] = low

        for z in range(nz):
            gather(1 + z, lambda slot, z=z: sites[sweep, slot, z])
        for copy in copies:
            copy.wait()
        gather(0, lambda slot: below[sweep, slot])
        for z in range(2):
            gather(3 + z, lambda slot, z=z: above[sweep, slot, z])
        for z in range(nz):
            product = [jnp.zeros((2 * HALF, 256), F32) for _ in range(nx)]
            for dy in range(3):
                right = rows[dy, :, z:z + 4].reshape(256, 256)
                left = jnp.concatenate([operator[x * nz + z, dy] for x in range(nx)], axis=0)
                whole = dot(left, right)
                for x in range(nx):
                    product[x] = product[x] + whole[2 * HALF * x:2 * HALF * (x + 1)]
            value = jnp.zeros((HALF, 128), F32)
            for x in range(nx):
                whole = product[x][:HALF, :128] + product[x][:HALF, 128:] + product[x][HALF:, :128]
                value = jnp.where(wide_part == x, whole, value)
            current[z] = start[z] + (current[z] - value)

    for z in range(nz):
        cells = dot(back_ref[...], joined_split(current[z]))
        store(result_ref, z, cells[:, :128] + cells[:, 128:])


def body(sizes, displacement, dof_weight, coarse_matrix, block_inverse):
    shape = displacement.shape
    cells = shape[0] * shape[1] * shape[2]
    edges = shape[3]
    rhs, dofs = shape[5], shape[6]
    coarse = block_inverse.shape[-1]
    consts = [jnp.asarray(t) for t in tables()]
    vmem = pl.BlockSpec(memory_space=pltpu.VMEM)
    hbm = pl.BlockSpec(memory_space=pl.ANY)
    average, result = pl.pallas_call(
        functools.partial(kernel, sizes),
        out_shape=[jax.ShapeDtypeStruct((cells, coarse, rhs), F32)] * 2,
        in_specs=[hbm, vmem, hbm] + [vmem] * 7,
        out_specs=[vmem, vmem],
        scratch_shapes=[
            pltpu.VMEM((cells, 3 * edges * rhs, dofs), BF16),
            pltpu.VMEM((27 * cells, coarse, coarse), F32),
            pltpu.VMEM((cells, 3, 2 * HALF, 256), BF16),
            pltpu.VMEM((3, 3, 16, 128), F32),
            pltpu.VMEM((9, 3, 16, 128), F32),
            pltpu.VMEM((3, 2, 16, 128), F32),
            pltpu.VMEM((2, 2, 16, 128), F32),
            pltpu.VMEM((SWEEPS - 1, 9, 2, 16, 128), F32),
            pltpu.VMEM((SWEEPS - 1, 9, 16, 128), F32),
            pltpu.VMEM((SWEEPS - 1, 9, 2, 16, 128), F32),
            pltpu.VMEM((3, 4, 5, 16, 256), BF16),
            pltpu.VMEM((64, 128), F32),
            pltpu.SemaphoreType.DMA((2,)),
            pltpu.SemaphoreType.DMA((SWEEPS, 13)),
            pltpu.SemaphoreType.DMA((SWEEPS, 13)),
        ],
        compiler_params=pltpu.CompilerParams(
            collective_id=0, has_side_effects=True, vmem_limit_bytes=40 * 1024 * 1024
        ),
    )(
        displacement.reshape(cells, 3 * edges * rhs, dofs),
        dof_weight.reshape(cells, edges, dofs),
        coarse_matrix.reshape(27 * cells, coarse, coarse),
        block_inverse.reshape(cells, coarse, coarse),
        *consts,
    )
    return (
        average.reshape(shape[:3] + (edges, 3, rhs)),
        result.reshape(shape[:3] + (coarse, rhs)),
    )


def solution(mesh):
    placed = (
        P("gx", "gy", "gz", None, None, None, None),
        P("gx", "gy", "gz", None, None),
        P("gx", "gy", "gz", None, None, None),
        P("gx", "gy", "gz", None, None),
    )
    sizes = tuple(mesh.shape[a] for a in ("gx", "gy", "gz"))
    return jax.shard_map(
        functools.partial(body, sizes),
        mesh=mesh,
        in_specs=placed,
        out_specs=(P("gx", "gy", "gz", None, None, None), P("gx", "gy", "gz", None, None)),
        check_vma=False,
    )
```

```python
import functools
import itertools

import jax
import jax.numpy as jnp
import ml_dtypes
import numpy as np
from jax import lax
from jax.experimental import pallas as pl
from jax.experimental.pallas import tpu as pltpu
from jax.sharding import PartitionSpec as P

SWEEPS = 4
MESH = pl.DeviceIdType.MESH
F32 = jnp.float32
BF16 = jnp.bfloat16
OFFSETS = [
    (0, 0, 0), (0, 0, 1), (0, 1, 0), (0, 1, 1),
    (0, 0, 0), (0, 0, 1), (1, 0, 0), (1, 0, 1),
    (0, 0, 0), (0, 1, 0), (1, 0, 0), (1, 1, 0),
]
STEPS = [(0, 0)] + [s for s in itertools.product((-1, 0, 1), (-1, 0, 1)) if s != (0, 0)]
SLOT = {s: i for i, s in enumerate(STEPS)}
HALF = 48
PAIR = 80


def site_row(edge, comp):
    oy = OFFSETS[edge][1]
    if edge < 4:
        return 3 * oy + comp
    if edge < 8:
        return (6, 7, 14)[comp]
    return 8 + 3 * oy + comp


def tables(nz):
    place = np.zeros((36 * nz, 64 * nz), np.float32)
    spread = np.zeros((nz, 64, 12 * nz), np.float32)
    chunk = np.full((64, 128), -1, np.int32)
    fold = np.zeros((3, 108, 256), np.float32)
    order = np.zeros((HALF, 36), np.float32)
    widen = np.zeros((2, nz, 36, 3 * PAIR), np.float32)
    rest = 16
    for edge in range(12):
        ox, oy, oz = OFFSETS[edge]
        for comp in range(3):
            row = 3 * edge + comp
            site = site_row(edge, comp)
            wide = 16 * (2 * ox + oz) + site
            chunk[wide] = row - np.arange(128) // 32
            for z in range(nz):
                place[nz * row + z, 64 * z + wide] = 1
                spread[z, wide, nz * edge + z] = 1
                widen[0, z, row, nz * row + z] = 1
                widen[1, z, row, PAIR + nz * row + z] = 1
                widen[0, z, row, 2 * PAIR + nz * row + z] = 1
            for dx in range(3):
                for dz in range(3):
                    fold[dx, 36 * dz + row, 64 * (dx + ox) + 16 * (dz + oz) + site] = 1
            if ox == 0 and oz == 0:
                order[site, row] = 1
            else:
                order[rest, row] = 1
                rest += 1
    kind = ml_dtypes.bfloat16
    return (place.astype(kind), spread.astype(kind), chunk, fold.astype(kind),
            order.astype(kind), widen.astype(kind))


def split(value):
    high = value.astype(BF16)
    return high, (value - high.astype(F32)).astype(BF16)


def dot(a, b):
    return jnp.dot(a, b, preferred_element_type=F32)


def kernel(sizes, disp_hbm, weight_ref, matrix_hbm, inverse_ref, place_ref, spread_ref, chunk_ref,
           fold_ref, order_ref, widen_ref, average_ref, result_ref,
           disp, matrix, operator, main, rim, zsend, zgot, sites, below, above, rows, wide, base, cells_ref,
           load_sem, send_sem, got_sem, pass_sem, passed_sem):
    nx, nz = 4, 2
    gx, gy, gz = (lax.axis_index(a) for a in ("gx", "gy", "gz"))
    cx, cy, cz = sizes

    def at(dx, dy, dz):
        return (lax.rem(gx + dx + cx, cx), lax.rem(gy + dy + cy, cy), lax.rem(gz + dz + cz, cz))

    load_disp = pltpu.make_async_copy(disp_hbm, disp, load_sem.at[0])
    load_matrix = pltpu.make_async_copy(matrix_hbm, matrix, load_sem.at[1])
    load_disp.start()
    load_matrix.start()
    barrier = pltpu.get_barrier_semaphore()
    for dx, dy in STEPS[1:]:
        pl.semaphore_signal(barrier, inc=1, device_id=at(dx, dy, 0), device_id_type=MESH)
    for dz in (-1, 1):
        pl.semaphore_signal(barrier, inc=1, device_id=at(0, 0, dz), device_id_type=MESH)

    lane = lax.broadcasted_iota(jnp.int32, (16, 128), 1)
    row = lax.broadcasted_iota(jnp.int32, (16, 128), 0)
    part = lane // 32
    ones = jnp.ones((128, 128), BF16)
    zero = jnp.zeros((16, 128), F32)

    load_disp.wait()
    number = {}
    mass = {}
    for cell in range(nx * nz):
        weight = dot(spread_ref[cell % nz], weight_ref[cell // nz]).astype(BF16)
        full = lax.dot_general(weight, disp[cell], (((1,), (1,)), ((), ())),
                               preferred_element_type=F32)
        total = jnp.zeros((64, 128), F32)
        for t in range(9):
            total = total + jnp.where(chunk_ref[...] == 4 * t, full[:, 128 * t:128 * t + 128], 0.0)
        total = total + pltpu.roll(total, 64, 1)
        total = total + pltpu.roll(total, 32, 1)
        number[cell] = total
        mass[cell] = dot(weight, ones)
    for zs in range(nz + 1):
        body = zero
        edge = zero
        for oz in range(2):
            z = zs - oz
            if not 0 <= z < nz:
                continue
            for x in range(nx):
                for ox in range(2):
                    b = 16 * (2 * ox + oz)
                    value = number[x * nz + z][b:b + 16]
                    if x + ox < nx:
                        body = body + jnp.where(part == x + ox, value, 0.0)
                    else:
                        edge = edge + jnp.where(part == 0, value, 0.0)
                    heavy = mass[x * nz + z][b:b + 16]
                    edge = edge + jnp.where(lane // 8 == 4 + x + ox, heavy, 0.0)
        main[1, zs] = body
        rim[0, zs] = edge + jnp.where(part == 3, pltpu.roll(body, 96, 1), 0.0)

    pl.semaphore_wait(barrier, 10)
    copies = []
    for i, (dx, dy) in enumerate(STEPS):
        if i == 0:
            continue
        slot = SLOT[(-dx, -dy)]
        copies.append(pltpu.make_async_remote_copy(
            rim.at[0], rim.at[slot], send_sem.at[0, i], got_sem.at[0, slot],
            device_id=at(dx, dy, 0), device_id_type=MESH))
        if dx == 0:
            copies.append(pltpu.make_async_remote_copy(
                main.at[1], main.at[1 - dy], send_sem.at[0, 11 + (dy + 1) // 2],
                got_sem.at[0, 11 + (1 - dy) // 2],
                device_id=at(dx, dy, 0), device_id_type=MESH))
    for copy in copies:
        copy.start()

    load_matrix.wait()

    def prepare(x, carry):
        wide_base = []
        for z in range(nz):
            high, low = split(inverse_ref[x, pl.ds(z, 36, stride=nz), :])
            high = dot(order_ref[...], high).astype(BF16)
            low = dot(order_ref[...], low).astype(BF16)
            base[z, x, :HALF] = high
            base[z, x, HALF:] = low
            wide_base.append(dot(high, widen_ref[0, z]) + dot(low, widen_ref[1, z]))
        wide_base = jnp.concatenate(wide_base, axis=0).astype(BF16)
        for dy in range(3):
            total = jnp.zeros((2 * PAIR, 256), F32)
            for dx in range(3):
                first = 27 * x + 9 * dx + 3 * dy
                joined = jnp.concatenate([matrix[first + k] for k in range(3)], axis=1)
                joined = jnp.concatenate([joined, jnp.zeros((PAIR - 36 * nz, 108), F32)], axis=0)
                total = total + dot(jnp.concatenate(split(joined), axis=0), fold_ref[dx])
            total = total.astype(BF16)
            total = jnp.concatenate([total[:PAIR], total[:PAIR], total[PAIR:]], axis=0)
            scaled = dot(wide_base, total)
            for z in range(nz):
                high, low = split(scaled[HALF * z:HALF * (z + 1)])
                operator[z, dy, x, :HALF] = high
                operator[z, dy, x, HALF:] = low
        return carry

    lax.fori_loop(0, nx, prepare, 0)

    for copy in copies:
        copy.wait()

    lower = (row % 8) < 3
    upper = ((row % 8) >= 3) & ((row % 8) < 6)
    for zs in range(nz + 1):
        sums = {}
        for dy in (-1, 0, 1):
            before = rim[SLOT[(-1, dy)], zs]
            after = pltpu.roll(rim[SLOT[(1, dy)], zs], 32, 1)
            body = main[1 + dy, zs] + jnp.where(part == 0, before, 0.0)
            edge = (rim[SLOT[(0, dy)], zs]
                    + jnp.where(lane // 8 == 4, pltpu.roll(before, 96, 1), 0.0)
                    + jnp.where((part == 0) | (lane // 8 == 8), after, 0.0))
            sums[dy] = (body, edge)
        for k in range(2):
            zsend[zs, k] = (sums[0][k]
                            + jnp.where(lower, pltpu.roll(sums[-1][k], 13, 0), 0.0)
                            + jnp.where(upper, pltpu.roll(sums[1][k], 3, 0), 0.0))
    copies = [
        pltpu.make_async_remote_copy(zsend.at[nz], zgot.at[0], send_sem.at[0, 9], got_sem.at[0, 9],
                                     device_id=at(0, 0, 1), device_id_type=MESH),
        pltpu.make_async_remote_copy(zsend.at[0], zgot.at[1], send_sem.at[0, 10], got_sem.at[0, 10],
                                     device_id=at(0, 0, -1), device_id_type=MESH),
    ]
    for copy in copies:
        copy.start()
    for copy in copies:
        copy.wait()
    inner = []
    outer = []
    for zs in range(nz + 1):
        body = zsend[zs, 0]
        edge = zsend[zs, 1]
        if zs == 0:
            body, edge = body + zgot[0, 0], edge + zgot[0, 1]
        if zs == nz:
            body, edge = body + zgot[1, 0], edge + zgot[1, 1]
        heavy = zero
        for x in range(nx):
            heavy = jnp.where(part == x, edge[:, 32 + 8 * x:33 + 8 * x], heavy)
        last = jnp.broadcast_to(edge[:, 64:65], (16, 128))
        inner.append(body / jnp.where(heavy == 0.0, 1.0, heavy))
        edge = edge / jnp.where(last == 0.0, 1.0, last)
        outer.append(jnp.where(part == 3, pltpu.roll(edge, 96, 1), pltpu.roll(inner[-1], 96, 1)))

    def joined_split(value):
        high, low = split(value)
        return jnp.concatenate([high, low], axis=1)

    wide_part = lax.broadcasted_iota(jnp.int32, (HALF, 128), 1) // 32
    start = []
    current = []
    for z in range(nz):
        wide[z] = jnp.concatenate([inner[z], inner[z + 1], outer[z], outer[z + 1]], axis=0)
    pair = joined_split(wide[...].reshape(64 * nz, 128))
    cells = dot(place_ref[...], pair)
    cells = cells[:, :128] + cells[:, 128:]
    for x in range(nx):
        average_ref[x] = cells[:, 32 * x:32 * x + 32]
    cells_ref[...] = cells
    for z in range(nz):
        right = joined_split(cells_ref[pl.ds(z, 36, stride=nz), :])
        whole = dot(base[z].reshape(2 * HALF * nx, 36), right)
        value = jnp.zeros((HALF, 128), F32)
        for x in range(nx):
            high = whole[2 * HALF * x:2 * HALF * x + HALF]
            low = whole[2 * HALF * x + HALF:2 * HALF * (x + 1)]
            value = jnp.where(wide_part == x, high[:, :128] + high[:, 128:] + low[:, :128], value)
        start.append(value)
        current.append(value)

    for sweep in range(SWEEPS - 1):
        r = sweep + 1
        for z in range(nz):
            sites[sweep, 0, z] = current[z][:16]
        copies = []
        for i, (dx, dy) in enumerate(STEPS):
            if i == 0:
                continue
            slot = SLOT[(-dx, -dy)]
            copies.append(pltpu.make_async_remote_copy(
                sites.at[sweep, 0], sites.at[sweep, slot], send_sem.at[r, i], got_sem.at[r, slot],
                device_id=at(dx, dy, 0), device_id_type=MESH))
        for copy in copies:
            copy.start()
        passing = []
        for i in range(9):
            if i > 0:
                slot = SLOT[(-STEPS[i][0], -STEPS[i][1])]
                copies[i - 1].wait_recv()
            else:
                slot = 0
            passing.append(pltpu.make_async_remote_copy(
                sites.at[sweep, slot], above.at[sweep, slot],
                pass_sem.at[0, sweep, slot], passed_sem.at[0, sweep, slot],
                device_id=at(0, 0, -1), device_id_type=MESH))
            passing[-1].start()
            if cz > 2:
                passing.append(pltpu.make_async_remote_copy(
                    sites.at[sweep, slot, nz - 1], below.at[sweep, slot],
                    pass_sem.at[1, sweep, slot], passed_sem.at[1, sweep, slot],
                    device_id=at(0, 0, 1), device_id_type=MESH))
                passing[-1].start()

        def gather(zs, load, sweep=sweep):
            for dy in (-1, 0, 1):
                own, before, after = (load(SLOT[(s, dy)]) for s in (0, -1, 1))
                shifted = [
                    jnp.where(part == 0, pltpu.roll(before, 32, 1), pltpu.roll(own, 32, 1)),
                    own,
                    jnp.where(part == 3, pltpu.roll(after, 96, 1), pltpu.roll(own, 96, 1)),
                    jnp.where(part >= 2, pltpu.roll(after, 64, 1), pltpu.roll(own, 64, 1)),
                ]
                for s in range(4):
                    high, low = split(shifted[s])
                    rows[dy + 1, s, zs, :, :128] = high
                    rows[dy + 1, s, zs, :, 128:] = low

        for z in range(nz):
            gather(1 + z, lambda slot, z=z: sites[sweep, slot, z])
        for copy in copies:
            copy.wait_send()
        for copy in passing:
            copy.wait()
        gather(0, lambda slot: below[sweep, slot] if cz > 2 else above[sweep, slot, nz - 1])
        for z in range(2):
            gather(3 + z, lambda slot, z=z: above[sweep, slot, z])
        for z in range(nz):
            product = [jnp.zeros((2 * HALF, 256), F32) for _ in range(nx)]
            for dy in range(3):
                right = rows[dy, :, z:z + 4].reshape(256, 256)
                left = operator[z, dy].reshape(2 * HALF * nx, 256)
                whole = dot(left, right)
                for x in range(nx):
                    product[x] = product[x] + whole[2 * HALF * x:2 * HALF * (x + 1)]
            value = jnp.zeros((HALF, 128), F32)
            for x in range(nx):
                whole = product[x][:HALF, :128] + product[x][:HALF, 128:] + product[x][HALF:, :128]
                value = jnp.where(wide_part == x, whole, value)
            current[z] = start[z] + (current[z] - value)

    for z in range(nz):
        high, low = (lax.dot_general(v, order_ref[...], (((0,), (0,)), ((), ())),
                                     preferred_element_type=F32) for v in split(current[z]))
        cells = high + low
        for x in range(nx):
            result_ref[x * nz + z] = cells[32 * x:32 * x + 32]


def body(sizes, displacement, dof_weight, coarse_matrix, block_inverse):
    shape = displacement.shape
    cells = shape[0] * shape[1] * shape[2]
    edges = shape[3]
    rhs, dofs = shape[5], shape[6]
    coarse = block_inverse.shape[-1]
    nx, nz = shape[0], shape[2]
    consts = [jnp.asarray(t) for t in tables(nz)]
    vmem = pl.BlockSpec(memory_space=pltpu.VMEM)
    hbm = pl.BlockSpec(memory_space=pl.ANY)
    average, result = pl.pallas_call(
        functools.partial(kernel, sizes),
        out_shape=[
            jax.ShapeDtypeStruct((nx, coarse * nz, rhs), F32),
            jax.ShapeDtypeStruct((cells, rhs, coarse), F32),
        ],
        in_specs=[hbm, vmem, hbm] + [vmem] * 7,
        out_specs=[vmem, vmem],
        scratch_shapes=[
            pltpu.VMEM((cells, 3 * edges * rhs, dofs), BF16),
            pltpu.VMEM((27 * nx, coarse * nz, coarse), F32),
            pltpu.VMEM((nz, 3, nx, 2 * HALF, 256), BF16),
            pltpu.VMEM((3, 3, 16, 128), F32),
            pltpu.VMEM((9, 3, 16, 128), F32),
            pltpu.VMEM((3, 2, 16, 128), F32),
            pltpu.VMEM((2, 2, 16, 128), F32),
            pltpu.VMEM((SWEEPS - 1, 9, 2, 16, 128), F32),
            pltpu.VMEM((SWEEPS - 1, 9, 16, 128), F32),
            pltpu.VMEM((SWEEPS - 1, 9, 2, 16, 128), F32),
            pltpu.VMEM((3, 4, 5, 16, 256), BF16),
            pltpu.VMEM((nz, 64, 128), F32),
            pltpu.VMEM((nz, nx, 2 * HALF, coarse), BF16),
            pltpu.VMEM((coarse * nz, 128), F32),
            pltpu.SemaphoreType.DMA((2,)),
            pltpu.SemaphoreType.DMA((SWEEPS, 13)),
            pltpu.SemaphoreType.DMA((SWEEPS, 13)),
            pltpu.SemaphoreType.DMA((2, SWEEPS - 1, 9)),
            pltpu.SemaphoreType.DMA((2, SWEEPS - 1, 9)),
        ],
        compiler_params=pltpu.CompilerParams(
            collective_id=0, has_side_effects=True, vmem_limit_bytes=60 * 1024 * 1024
        ),
    )(
        displacement.reshape(cells, 3 * edges * rhs, dofs),
        dof_weight.transpose(0, 1, 3, 2, 4).reshape(nx, edges * nz, dofs),
        coarse_matrix.transpose(0, 1, 3, 4, 2, 5).reshape(27 * nx, coarse * nz, coarse),
        block_inverse.transpose(0, 1, 3, 2, 4).reshape(nx, coarse * nz, coarse),
        *consts,
    )
    return (
        average.reshape(nx, 1, edges, 3, nz, rhs).transpose(0, 1, 4, 2, 3, 5),
        result.reshape(shape[:3] + (rhs, coarse)).transpose(0, 1, 2, 4, 3),
    )


def solution(mesh):
    placed = (
        P("gx", "gy", "gz", None, None, None, None),
        P("gx", "gy", "gz", None, None),
        P("gx", "gy", "gz", None, None, None),
        P("gx", "gy", "gz", None, None),
    )
    sizes = tuple(mesh.shape[a] for a in ("gx", "gy", "gz"))
    return jax.shard_map(
        functools.partial(body, sizes),
        mesh=mesh,
        in_specs=placed,
        out_specs=(P("gx", "gy", "gz", None, None, None), P("gx", "gy", "gz", None, None)),
        check_vma=False,
    )
```

```python
import functools
import itertools

import jax
import jax.numpy as jnp
import ml_dtypes
import numpy as np
from jax import lax
from jax.experimental import pallas as pl
from jax.experimental.pallas import tpu as pltpu
from jax.sharding import PartitionSpec as P

SWEEPS = 4
MESH = pl.DeviceIdType.MESH
F32 = jnp.float32
BF16 = jnp.bfloat16
OFFSETS = [
    (0, 0, 0), (0, 0, 1), (0, 1, 0), (0, 1, 1),
    (0, 0, 0), (0, 0, 1), (1, 0, 0), (1, 0, 1),
    (0, 0, 0), (0, 1, 0), (1, 0, 0), (1, 1, 0),
]
STEPS = [(0, 0), (-1, 0), (1, 0)] + [(dx, dy) for dy, dx in itertools.product((-1, 1), (-1, 0, 1))]
SLOT = {s: i for i, s in enumerate(STEPS)}
HALF = 48
PAIR = 80


def site_row(edge, comp):
    oy = OFFSETS[edge][1]
    if edge < 4:
        return 3 * oy + comp
    if edge < 8:
        return (6, 7, 14)[comp]
    return 8 + 3 * oy + comp


def tables(nz):
    place = np.zeros((36 * nz, 64 * nz), np.float32)
    spread = np.zeros((nz, 64, 12 * nz), np.float32)
    chunk = np.full((64, 128), -1, np.int32)
    fold = np.zeros((3, 108, 256), np.float32)
    order = np.zeros((HALF, 36), np.float32)
    widen = np.zeros((2, nz, 36, 3 * PAIR), np.float32)
    rest = 16
    for edge in range(12):
        ox, oy, oz = OFFSETS[edge]
        for comp in range(3):
            row = 3 * edge + comp
            site = site_row(edge, comp)
            wide = 16 * (2 * ox + oz) + site
            chunk[wide] = row - np.arange(128) // 32
            for z in range(nz):
                place[nz * row + z, 64 * z + wide] = 1
                spread[z, wide, nz * edge + z] = 1
                widen[0, z, row, nz * row + z] = 1
                widen[1, z, row, PAIR + nz * row + z] = 1
                widen[0, z, row, 2 * PAIR + nz * row + z] = 1
            for dx in range(3):
                for dz in range(3):
                    fold[dx, 36 * dz + row, 64 * (dx + ox) + 16 * (dz + oz) + site] = 1
            if ox == 0 and oz == 0:
                order[site, row] = 1
            else:
                order[rest, row] = 1
                rest += 1
    kind = ml_dtypes.bfloat16
    return (place.astype(kind), spread.astype(kind), chunk, fold.astype(kind),
            order.astype(kind), widen.astype(kind))


def split(value):
    high = value.astype(BF16)
    return high, (value - high.astype(F32)).astype(BF16)


def dot(a, b):
    return jnp.dot(a, b, preferred_element_type=F32)


def kernel(sizes, disp_hbm, weight_hbm, matrix_hbm, inverse_hbm, place_hbm, spread_hbm, chunk_hbm,
           fold_hbm, order_hbm, widen_hbm, average_ref, result_ref,
           weight_ref, inverse_ref, place_ref, spread_ref, chunk_ref, fold_ref, order_ref, widen_ref,
           disp, matrix, operator, main, rim, pack, zsend, zgot, sites, below, above, rows, wide, base, cells_ref,
           load_sem, send_sem, got_sem, pass_sem, passed_sem):
    nx, nz = 4, 2
    gx, gy, gz = (lax.axis_index(a) for a in ("gx", "gy", "gz"))
    cx, cy, cz = sizes

    def at(dx, dy, dz):
        return (lax.rem(gx + dx + cx, cx), lax.rem(gy + dy + cy, cy), lax.rem(gz + dz + cz, cz))

    load_disp = pltpu.make_async_copy(disp_hbm, disp, load_sem.at[0])
    load_matrix = pltpu.make_async_copy(matrix_hbm, matrix, load_sem.at[1])
    early = [pltpu.make_async_copy(a, b, load_sem.at[2 + i]) for i, (a, b) in enumerate(
        ((weight_hbm, weight_ref), (spread_hbm, spread_ref), (chunk_hbm, chunk_ref)))]
    late = [pltpu.make_async_copy(a, b, load_sem.at[5 + i]) for i, (a, b) in enumerate(
        ((inverse_hbm, inverse_ref), (place_hbm, place_ref), (fold_hbm, fold_ref),
         (order_hbm, order_ref), (widen_hbm, widen_ref)))]
    for copy in early:
        copy.start()
    load_disp.start()
    for copy in late:
        copy.start()
    load_matrix.start()
    barrier = pltpu.get_barrier_semaphore()
    for dx, dy in STEPS[1:]:
        pl.semaphore_signal(barrier, inc=1, device_id=at(dx, dy, 0), device_id_type=MESH)
    for dz in (-1, 1):
        pl.semaphore_signal(barrier, inc=1, device_id=at(0, 0, dz), device_id_type=MESH)

    lane = lax.broadcasted_iota(jnp.int32, (16, 128), 1)
    row = lax.broadcasted_iota(jnp.int32, (16, 128), 0)
    part = lane // 32
    ones = jnp.ones((128, 128), BF16)
    zero = jnp.zeros((16, 128), F32)
    few = row[:8] < 3
    next_few = (row[:8] >= 3) & (row[:8] < 6)

    for copy in early:
        copy.wait()
    load_disp.wait()
    number = {}
    mass = {}
    for cell in range(nx * nz):
        weight = dot(spread_ref[cell % nz], weight_ref[cell // nz]).astype(BF16)
        full = lax.dot_general(weight, disp[cell], (((1,), (1,)), ((), ())),
                               preferred_element_type=F32)
        total = jnp.zeros((64, 128), F32)
        for t in range(9):
            total = total + jnp.where(chunk_ref[...] == 4 * t, full[:, 128 * t:128 * t + 128], 0.0)
        total = total + pltpu.roll(total, 64, 1)
        total = total + pltpu.roll(total, 32, 1)
        number[cell] = total
        mass[cell] = dot(weight, ones)
    for zs in range(nz + 1):
        body = zero
        edge = zero
        for oz in range(2):
            z = zs - oz
            if not 0 <= z < nz:
                continue
            for x in range(nx):
                for ox in range(2):
                    b = 16 * (2 * ox + oz)
                    value = number[x * nz + z][b:b + 16]
                    if x + ox < nx:
                        body = body + jnp.where(part == x + ox, value, 0.0)
                    else:
                        edge = edge + jnp.where(part == 0, value, 0.0)
                    heavy = mass[x * nz + z][b:b + 16]
                    edge = edge + jnp.where(lane // 8 == 4 + x + ox, heavy, 0.0)
        main[1, zs] = body
        edge = edge + jnp.where(part == 3, pltpu.roll(body, 96, 1), 0.0)
        rim[0, zs] = edge
        for k, value in enumerate((body, edge)):
            first, second = value[:8], value[8:]
            pack[0, k, zs] = jnp.where(few, first, pltpu.roll(second, 3, 0))
            pack[1, k, zs] = jnp.where(few, pltpu.roll(first, 5, 0), second)

    pl.semaphore_wait(barrier, 10)
    copies = []
    for i, (dx, dy) in enumerate(STEPS):
        if i == 0:
            continue
        slot = SLOT[(-dx, -dy)]
        packed = (dy + 1) // 2
        copies.append(pltpu.make_async_remote_copy(
            pack.at[packed, 1] if dy else rim.at[0],
            rim.at[slot, :, pl.ds(0, 8)] if dy else rim.at[slot],
            send_sem.at[0, i], got_sem.at[0, slot],
            device_id=at(dx, dy, 0), device_id_type=MESH))
        if dx == 0 and dy:
            copies.append(pltpu.make_async_remote_copy(
                pack.at[packed, 0], main.at[1 - dy, :, pl.ds(0, 8)], send_sem.at[0, 11 + packed],
                got_sem.at[0, 12 - packed],
                device_id=at(dx, dy, 0), device_id_type=MESH))
    for copy in copies:
        copy.start()

    for copy in late:
        copy.wait()
    load_matrix.wait()

    def prepare(x, carry):
        wide_base = []
        for z in range(nz):
            high, low = split(inverse_ref[x, pl.ds(z, 36, stride=nz), :])
            high = dot(order_ref[...], high).astype(BF16)
            low = dot(order_ref[...], low).astype(BF16)
            base[z, x, :HALF] = high
            base[z, x, HALF:] = low
            wide_base.append(dot(high, widen_ref[0, z]) + dot(low, widen_ref[1, z]))
        wide_base = jnp.concatenate(wide_base, axis=0).astype(BF16)
        for dy in range(3):
            total = jnp.zeros((2 * PAIR, 256), F32)
            for dx in range(3):
                first = 27 * x + 9 * dx + 3 * dy
                joined = jnp.concatenate([matrix[first + k] for k in range(3)], axis=1)
                joined = jnp.concatenate([joined, jnp.zeros((PAIR - 36 * nz, 108), F32)], axis=0)
                total = total + dot(jnp.concatenate(split(joined), axis=0), fold_ref[dx])
            total = total.astype(BF16)
            total = jnp.concatenate([total[:PAIR], total[:PAIR], total[PAIR:]], axis=0)
            scaled = dot(wide_base, total)
            for z in range(nz):
                high, low = split(scaled[HALF * z:HALF * (z + 1)])
                operator[z, dy, x, :HALF] = high
                operator[z, dy, x, HALF:] = low
        return carry

    lax.fori_loop(0, nx, prepare, 0)

    for copy in copies:
        copy.wait()

    for zs in range(nz + 1):
        sums = {}
        for dy in (-1, 0, 1):
            count = 8 if dy else 16
            spot, eighth = part[:count], lane[:count] // 8
            before = rim[SLOT[(-1, dy)], zs, :count]
            after = pltpu.roll(rim[SLOT[(1, dy)], zs, :count], 32, 1)
            body = main[1 + dy, zs, :count] + jnp.where(spot == 0, before, 0.0)
            edge = (rim[SLOT[(0, dy)], zs, :count]
                    + jnp.where(eighth == 4, pltpu.roll(before, 96, 1), 0.0)
                    + jnp.where((spot == 0) | (eighth == 8), after, 0.0))
            sums[dy] = (body, edge)
        for k in range(2):
            low, high = sums[-1][k], sums[1][k]
            zsend[zs, k] = sums[0][k] + jnp.concatenate([
                jnp.where(few, low, jnp.where(next_few, pltpu.roll(high, 3, 0), 0.0)),
                jnp.where(few, pltpu.roll(low, 5, 0), jnp.where(next_few, high, 0.0)),
            ], axis=0)
    copies = [
        pltpu.make_async_remote_copy(zsend.at[nz], zgot.at[0], send_sem.at[0, 9], got_sem.at[0, 9],
                                     device_id=at(0, 0, 1), device_id_type=MESH),
        pltpu.make_async_remote_copy(zsend.at[0], zgot.at[1], send_sem.at[0, 10], got_sem.at[0, 10],
                                     device_id=at(0, 0, -1), device_id_type=MESH),
    ]
    for copy in copies:
        copy.start()
    for copy in copies:
        copy.wait()
    inner = []
    outer = []
    for zs in range(nz + 1):
        body = zsend[zs, 0]
        edge = zsend[zs, 1]
        if zs == 0:
            body, edge = body + zgot[0, 0], edge + zgot[0, 1]
        if zs == nz:
            body, edge = body + zgot[1, 0], edge + zgot[1, 1]
        heavy = zero
        for x in range(nx):
            heavy = jnp.where(part == x, edge[:, 32 + 8 * x:33 + 8 * x], heavy)
        last = jnp.broadcast_to(edge[:, 64:65], (16, 128))
        inner.append(body / jnp.where(heavy == 0.0, 1.0, heavy))
        edge = edge / jnp.where(last == 0.0, 1.0, last)
        outer.append(jnp.where(part == 3, pltpu.roll(edge, 96, 1), pltpu.roll(inner[-1], 96, 1)))

    def joined_split(value):
        high, low = split(value)
        return jnp.concatenate([high, low], axis=1)

    wide_part = lax.broadcasted_iota(jnp.int32, (HALF, 128), 1) // 32
    start = []
    current = []
    for z in range(nz):
        wide[z] = jnp.concatenate([inner[z], inner[z + 1], outer[z], outer[z + 1]], axis=0)
    pair = joined_split(wide[...].reshape(64 * nz, 128))
    cells = dot(place_ref[...], pair)
    cells = cells[:, :128] + cells[:, 128:]
    for x in range(nx):
        average_ref[x] = cells[:, 32 * x:32 * x + 32]
    cells_ref[...] = cells
    for z in range(nz):
        right = joined_split(cells_ref[pl.ds(z, 36, stride=nz), :])
        whole = dot(base[z].reshape(2 * HALF * nx, 36), right)
        value = jnp.zeros((HALF, 128), F32)
        for x in range(nx):
            high = whole[2 * HALF * x:2 * HALF * x + HALF]
            low = whole[2 * HALF * x + HALF:2 * HALF * (x + 1)]
            value = jnp.where(wide_part == x, high[:, :128] + high[:, 128:] + low[:, :128], value)
        start.append(value)
        current.append(value)

    for sweep in range(SWEEPS - 1):
        r = sweep + 1
        for z in range(nz):
            sites[sweep, 0, z] = current[z][:16]
        coming = {}
        for i in (*range(3, 9), 1, 2):
            dx, dy = STEPS[i]
            slot = SLOT[(-dx, -dy)]
            coming[slot] = pltpu.make_async_remote_copy(
                sites.at[sweep, 0], sites.at[sweep, slot], send_sem.at[r, i], got_sem.at[r, slot],
                device_id=at(dx, dy, 0), device_id_type=MESH)
            coming[slot].start()
        passing = {}

        def forward(slot):
            if slot > 0:
                coming[slot].wait_recv()
            passing[slot] = [pltpu.make_async_remote_copy(
                sites.at[sweep, slot], above.at[sweep, slot],
                pass_sem.at[0, sweep, slot], passed_sem.at[0, sweep, slot],
                device_id=at(0, 0, -1), device_id_type=MESH)]
            if cz > 2:
                passing[slot].append(pltpu.make_async_remote_copy(
                    sites.at[sweep, slot, nz - 1], below.at[sweep, slot],
                    pass_sem.at[1, sweep, slot], passed_sem.at[1, sweep, slot],
                    device_id=at(0, 0, 1), device_id_type=MESH))
            for copy in passing[slot]:
                copy.start()

        def gather(dy, zs, load):
            own, before, after = (load(SLOT[(s, dy)]) for s in (0, -1, 1))
            shifted = [
                jnp.where(part == 0, pltpu.roll(before, 32, 1), pltpu.roll(own, 32, 1)),
                own,
                jnp.where(part == 3, pltpu.roll(after, 96, 1), pltpu.roll(own, 96, 1)),
                jnp.where(part >= 2, pltpu.roll(after, 64, 1), pltpu.roll(own, 64, 1)),
            ]
            for s in range(4):
                high, low = split(shifted[s])
                rows[dy + 1, s, zs, :, :128] = high
                rows[dy + 1, s, zs, :, 128:] = low

        def gather_all(dy):
            for z in range(nz):
                gather(dy, 1 + z, lambda slot: sites[sweep, slot, z])
            for s in (0, -1, 1):
                for copy in passing[SLOT[(s, dy)]]:
                    copy.wait_recv()
            gather(dy, 0, lambda slot: below[sweep, slot] if cz > 2 else above[sweep, slot, nz - 1])
            for z in range(2):
                gather(dy, 3 + z, lambda slot: above[sweep, slot, z])

        def multiply(z, dy):
            left = operator[z, dy + 1].reshape(2 * HALF * nx, 256)
            return dot(left, rows[dy + 1, :, z:z + 4].reshape(256, 256))

        for slot in range(3):
            forward(slot)
        gather_all(0)
        products = [multiply(z, 0) for z in range(nz)]
        for slot in range(3, 9):
            forward(slot)
        for dy in (-1, 1):
            gather_all(dy)
            products = [products[z] + multiply(z, dy) for z in range(nz)]
        for slot in range(9):
            if slot > 0:
                coming[slot].wait_send()
            for copy in passing[slot]:
                copy.wait_send()
        for z in range(nz):
            product = [products[z][2 * HALF * x:2 * HALF * (x + 1)] for x in range(nx)]
            value = jnp.zeros((HALF, 128), F32)
            for x in range(nx):
                whole = product[x][:HALF, :128] + product[x][:HALF, 128:] + product[x][HALF:, :128]
                value = jnp.where(wide_part == x, whole, value)
            current[z] = start[z] + (current[z] - value)

    for z in range(nz):
        high, low = (lax.dot_general(v, order_ref[...], (((0,), (0,)), ((), ())),
                                     preferred_element_type=F32) for v in split(current[z]))
        cells = high + low
        for x in range(nx):
            result_ref[x * nz + z] = cells[32 * x:32 * x + 32]


def body(sizes, displacement, dof_weight, coarse_matrix, block_inverse):
    shape = displacement.shape
    cells = shape[0] * shape[1] * shape[2]
    edges = shape[3]
    rhs, dofs = shape[5], shape[6]
    coarse = block_inverse.shape[-1]
    nx, nz = shape[0], shape[2]
    consts = [jnp.asarray(t) for t in tables(nz)]
    vmem = pl.BlockSpec(memory_space=pltpu.VMEM)
    hbm = pl.BlockSpec(memory_space=pl.ANY)
    average, result = pl.pallas_call(
        functools.partial(kernel, sizes),
        out_shape=[
            jax.ShapeDtypeStruct((nx, coarse * nz, rhs), F32),
            jax.ShapeDtypeStruct((cells, rhs, coarse), F32),
        ],
        in_specs=[hbm] * 10,
        out_specs=[vmem, vmem],
        scratch_shapes=[
            pltpu.VMEM((nx, edges * nz, dofs), BF16),
            pltpu.VMEM((nx, coarse * nz, coarse), F32),
            *[pltpu.VMEM(t.shape, t.dtype) for t in consts],
            pltpu.VMEM((cells, 3 * edges * rhs, dofs), BF16),
            pltpu.VMEM((27 * nx, coarse * nz, coarse), F32),
            pltpu.VMEM((nz, 3, nx, 2 * HALF, 256), BF16),
            pltpu.VMEM((3, 3, 16, 128), F32),
            pltpu.VMEM((9, 3, 16, 128), F32),
            pltpu.VMEM((2, 2, 3, 8, 128), F32),
            pltpu.VMEM((3, 2, 16, 128), F32),
            pltpu.VMEM((2, 2, 16, 128), F32),
            pltpu.VMEM((SWEEPS - 1, 9, 2, 16, 128), F32),
            pltpu.VMEM((SWEEPS - 1, 9, 16, 128), F32),
            pltpu.VMEM((SWEEPS - 1, 9, 2, 16, 128), F32),
            pltpu.VMEM((3, 4, 5, 16, 256), BF16),
            pltpu.VMEM((nz, 64, 128), F32),
            pltpu.VMEM((nz, nx, 2 * HALF, coarse), BF16),
            pltpu.VMEM((coarse * nz, 128), F32),
            pltpu.SemaphoreType.DMA((10,)),
            pltpu.SemaphoreType.DMA((SWEEPS, 13)),
            pltpu.SemaphoreType.DMA((SWEEPS, 13)),
            pltpu.SemaphoreType.DMA((2, SWEEPS - 1, 9)),
            pltpu.SemaphoreType.DMA((2, SWEEPS - 1, 9)),
        ],
        compiler_params=pltpu.CompilerParams(
            collective_id=0, has_side_effects=True, vmem_limit_bytes=60 * 1024 * 1024
        ),
    )(
        displacement.reshape(cells, 3 * edges * rhs, dofs),
        dof_weight.transpose(0, 1, 3, 2, 4).reshape(nx, edges * nz, dofs),
        coarse_matrix.transpose(0, 1, 3, 4, 2, 5).reshape(27 * nx, coarse * nz, coarse),
        block_inverse.transpose(0, 1, 3, 2, 4).reshape(nx, coarse * nz, coarse),
        *consts,
    )
    return (
        average.reshape(nx, 1, edges, 3, nz, rhs).transpose(0, 1, 4, 2, 3, 5),
        result.reshape(shape[:3] + (rhs, coarse)).transpose(0, 1, 2, 4, 3),
    )


def solution(mesh):
    placed = (
        P("gx", "gy", "gz", None, None, None, None),
        P("gx", "gy", "gz", None, None),
        P("gx", "gy", "gz", None, None, None),
        P("gx", "gy", "gz", None, None),
    )
    sizes = tuple(mesh.shape[a] for a in ("gx", "gy", "gz"))
    return jax.shard_map(
        functools.partial(body, sizes),
        mesh=mesh,
        in_specs=placed,
        out_specs=(P("gx", "gy", "gz", None, None, None), P("gx", "gy", "gz", None, None)),
        check_vma=False,
    )
```
